32 devices in a mesh: group: 2 (over y), seq: 16 (over z, x, core).
Axes of the slice: x: 2, y: 2, z: 4, core: 2. Of those that a mesh axis runs over, the one named last changes fastest.
Arguments:
- node_feats: bfloat16 [16384, 1024], P(('group', 'seq')), parts along dimension 0, may hold values from -6 to 6
- struct_feats: float32 [16384, 128], P(('group', 'seq')), parts along dimension 0, may hold values from -6 to 6
- op_blocks: float32 [256, 3, 64, 64], P(('group', 'seq')), parts along dimension 0, may hold values from -0.07 to 0.07
- laplace_index: int32 [256, 3], P(('group', 'seq')), parts along dimension 0, may hold values from 0 to 127, as said below
- graph_links: int32 [256, 3], P(('group', 'seq')), parts along dimension 0, may hold values from 0 to 127, as said below
- expander_slot: int32 [256, 4], P(('group', 'seq')), parts along dimension 0, may hold values from 0 to 7
- series_coef: float32 [9], replicated, may hold values from 0.3 to 1
- encode_weight: bfloat16 [128, 1024], replicated, may hold values from -0.5 to 0.5
- qkv_weight: bfloat16 [1024, 3072], replicated, may hold values from -0.1875 to 0.1875
- out_weight: bfloat16 [1024, 1024], replicated, may hold values from -0.1875 to 0.1875
Outputs:
- mixed: bfloat16 [16384, 1024], P(('group', 'seq')), parts along dimension 0
The draws below stay inside these ranges and needn't reach their ends.
There are 2 independent parts, one for each index of `group`. The reference program is written for one: setup_inputs(seed, part) draws one part's arguments, and reference() takes and returns one part's arrays. A program takes and returns all parts, laid end to end along the dimension named above; an argument that names none is the same for every part. Nothing has to cross between parts.
Inputs may be any that keep to these rules, and one draw needn't show every extreme that they name: `laplace_index`: each entry lies within 2 blocks of its row's block. `graph_links`: each entry lies within 2 blocks of its row's block.
All inputs are finite; a program needn't handle non-finite values.
Results may differ from the reference program's by a relative error of at most 0.012.
The reference program's roundings to bfloat16 on the way count: a program that leaves them out, or rounds other values in their place, can miss the bound.
Values may be sent and summed in bfloat16 or wider, within the bound.
A program may use at most 192 MiB of HBM per device.

```python
import jax
import jax.numpy as jnp
from jax import lax

D = 1024
HEADS = 16
HD = 64
PCH = 128
BS = 64
BLK_DEV = 8
DEG = 8
NGL = 3
NEXP = 4
REACH = 2
NBLK = 128
NODES = 8192
N_SEQ = 16


def neighbor_blocks(key, columns):
    offsets = jax.random.randint(key, (NBLK, columns), -REACH, REACH + 1)
    offsets = offsets.at[0, 0].set(0)
    offsets = offsets.at[NBLK - 1, 0].set(0)
    blocks = jnp.arange(NBLK, dtype=jnp.int32)[:, None] + offsets
    return jnp.clip(blocks, 0, NBLK - 1).astype(jnp.int32)


def laplace_links(key):
    block_ids = jnp.arange(NBLK, dtype=jnp.int32)
    present = jax.random.randint(jax.random.fold_in(key, 31), (NBLK,), 0, 16) != 0
    forward = jnp.logical_and(present, block_ids + REACH < NBLK)
    backward = jnp.concatenate([jnp.zeros((REACH,), dtype=jnp.bool_), forward[:NBLK - REACH]])
    offsets = jax.random.randint(jax.random.fold_in(key, 37), (NBLK, 3), -REACH, REACH + 1)
    spare = jnp.clip(block_ids[:, None] + offsets, 0, NBLK - 1).astype(jnp.int32)
    first = jnp.where(forward, block_ids + REACH, spare[:, 0])
    second = jnp.where(backward, block_ids - REACH, spare[:, 1])
    stacked = jnp.stack([first, second, spare[:, 2]], axis=1).astype(jnp.int32)
    rotate = jax.random.randint(jax.random.fold_in(key, 41), (NBLK,), 0, 3)
    order = ((jnp.arange(3, dtype=jnp.int32)[None, :] + rotate[:, None]) % 3).astype(jnp.int32)
    return (forward, backward, order, jnp.take_along_axis(stacked, order, axis=1).astype(jnp.int32))


def draw_laplace_index(key, part):
    return laplace_links(jax.random.fold_in(key, 11))[3]


def draw_op_blocks(key, part):
    base = jax.random.fold_in(key, 11)
    forward, backward, order, index = laplace_links(base)
    block_keys = jax.random.split(jax.random.fold_in(base, 43), NBLK)
    perms = jax.vmap(lambda seed_key: jax.random.permutation(seed_key, BS))(block_keys).astype(jnp.int32)
    columns = jnp.arange(BS, dtype=jnp.int32)
    intersection = jnp.bitwise_and(perms[:, :, None], columns[None, None, :])
    parity = jnp.zeros_like(intersection)
    for level in range(BS.bit_length() - 1):
        parity = parity + jnp.bitwise_and(jnp.right_shift(intersection, level), 1)
    hadamard = (1 - 2 * (parity % 2)).astype(jnp.float32) / BS ** 0.5
    row_sign = (jax.random.randint(jax.random.fold_in(base, 47), (NBLK, BS), 0, 2) * 2 - 1).astype(jnp.float32)
    col_sign = (jax.random.randint(jax.random.fold_in(base, 53), (NBLK, BS), 0, 2) * 2 - 1).astype(jnp.float32)
    rotated = row_sign[:, :, None] * col_sign[:, None, :] * hadamard
    noise = jnp.clip(jax.random.normal(jax.random.fold_in(base, 59), (NBLK, 4, BS, BS), jnp.float32), -4.0, 4.0)
    linked = 0.43 * (rotated + 0.00625 * noise[:, 0])
    flipped = jnp.swapaxes(linked, 1, 2)
    behind = jnp.concatenate([jnp.zeros((REACH, BS, BS), jnp.float32), flipped[:NBLK - REACH]], axis=0)
    spare = 0.0025 * noise[:, 1:]
    first = jnp.where(forward[:, None, None], linked, spare[:, 0])
    second = jnp.where(backward[:, None, None], behind, spare[:, 1])
    stacked = jnp.stack([first, second, spare[:, 2]], axis=1)
    return jnp.take_along_axis(stacked, order[:, :, None, None], axis=1).astype(jnp.float32)


def draw_graph_links(key, part):
    return neighbor_blocks(jax.random.fold_in(key, 23), NGL)


def plant(values, own_key, least, top_value):
    dims = values.shape
    place = [jax.random.randint(jax.random.fold_in(own_key, axis), (), 0, dims[axis]) for axis in range(len(dims))]
    values = values.at[tuple(place)].set(least)
    longest = dims.index(max(dims))
    place[longest] = (place[longest] + 1) % dims[longest]
    return values.at[tuple(place)].set(top_value)


def level_of(stream_key, shape, shards, smallest, largest):
    gain, own = 1.0, jax.random.fold_in(stream_key, 6)
    for dim, shards_of in shards:
        steps = jnp.exp(jax.random.uniform(jax.random.fold_in(own, dim), (shards_of,), jnp.float32, smallest / len(shards), largest / len(shards)))
        gain = gain * jnp.repeat(steps, shape[dim] // shards_of).reshape([-1 if axis == dim else 1 for axis in range(len(shape))])
    return gain


def normal_values(stream_key, dims, width, limit, shards=(), held_as=jnp.bfloat16):
    values = jax.random.normal(stream_key, dims, jnp.float32) * width
    if len(shards) > 0:
        values = level_of(stream_key, dims, shards, -0.22, 0.18) * values
    return jnp.clip(values, min=-limit, max=limit).astype(held_as)


def setup_inputs(seed: int = 0, part: int = 0) -> dict:
    key_list = jax.random.split(jax.random.key(seed), 11)
    part_splits = jax.random.split(jax.random.fold_in(key_list[10], part), 11)
    return {
        "node_feats": normal_values(part_splits[0], (NODES, D), 1.0, 6.0, ((0, 16),)),
        "struct_feats": normal_values(part_splits[1], (NODES, PCH), 1.0, 6.0, ((0, 16),), jnp.float32),
        "op_blocks": draw_op_blocks(jax.random.fold_in(jax.random.fold_in(key_list[10], part), 71), part),
        "laplace_index": draw_laplace_index(jax.random.fold_in(jax.random.fold_in(key_list[10], part), 71), part),
        "graph_links": draw_graph_links(jax.random.fold_in(jax.random.fold_in(key_list[10], part), 71), part),
        "expander_slot": plant(jax.random.randint(part_splits[5], (NBLK, NEXP), 0, BLK_DEV), jax.random.fold_in(part_splits[5], 1), 0, BLK_DEV - 1).astype(jnp.int32),
        "series_coef": jnp.clip(jax.random.uniform(key_list[6], (DEG + 1,), jnp.float32, 0.3, 1.0), 0.3, 1.0),
        "encode_weight": normal_values(key_list[7], (PCH, D), PCH ** -0.5, 0.5),
        "qkv_weight": normal_values(key_list[8], (D, 3 * D), D ** -0.5, 0.1875),
        "out_weight": normal_values(key_list[9], (D, D), D ** -0.5, 0.1875),
    }


def apply_operator(field, op_blocks, laplace_index):
    count = op_blocks.shape[0]
    blocks = field.reshape(count, BS, field.shape[1])
    picked = blocks[laplace_index]
    result = jnp.einsum("bjst,bjtc->bsc", op_blocks, picked, precision=lax.Precision.HIGHEST)
    return result.reshape(field.shape)


def attend_block(query_block, picked):
    scale = 1.0 / (HD ** 0.5)
    keys = picked[:, :D].astype(jnp.float32).reshape(-1, HEADS, HD)
    values = picked[:, D:].astype(jnp.float32).reshape(-1, HEADS, HD)
    qheads = query_block.astype(jnp.float32).reshape(-1, HEADS, HD)
    scores = jnp.einsum("qhd,khd->hqk", qheads, keys) * scale
    weights = jax.nn.softmax(scores, axis=-1).astype(jnp.bfloat16)
    result = jnp.einsum("hqk,khd->qhd", weights.astype(jnp.float32), values)
    return result.reshape(-1, D).astype(jnp.bfloat16)


def reference(node_feats, struct_feats, op_blocks, laplace_index, graph_links, expander_slot, series_coef, encode_weight, qkv_weight, out_weight):
    previous = struct_feats
    current = apply_operator(previous, op_blocks, laplace_index)
    encoding = series_coef[0] * previous + series_coef[1] * current
    for degree in range(2, DEG + 1):
        following = 2.0 * apply_operator(current, op_blocks, laplace_index) - previous
        encoding = encoding + series_coef[degree] * following
        previous, current = current, following
    encoded = jnp.dot(encoding.astype(jnp.bfloat16), encode_weight, preferred_element_type=jnp.float32)
    blended = (node_feats.astype(jnp.float32) + encoded).astype(jnp.bfloat16)
    projected = jnp.dot(blended, qkv_weight, preferred_element_type=jnp.float32)
    queries = projected[:, :D].astype(jnp.bfloat16)
    keyvals = projected[:, D:].astype(jnp.bfloat16)
    count = laplace_index.shape[0]
    levels = N_SEQ.bit_length() - 1
    block_ids = jnp.arange(count, dtype=jnp.int32)
    device_of = block_ids // BLK_DEV
    bit_values = jnp.array([1 << (link * (levels - 1) // (NEXP - 1)) for link in range(NEXP)], dtype=jnp.int32)
    partner = jnp.bitwise_xor(device_of[:, None], bit_values[None, :])
    far_blocks = (partner * BLK_DEV + expander_slot).astype(jnp.int32)
    key_index = jnp.concatenate([block_ids[:, None], graph_links.astype(jnp.int32), far_blocks], axis=1).astype(jnp.int32)
    kv_blocks = keyvals.reshape(count, BS, 2 * D)
    query_blocks = queries.reshape(count, BS, D)

    def one_block(item):
        query_block, row = item
        picked = kv_blocks[row].reshape(-1, 2 * D)
        return attend_block(query_block, picked)

    attended = lax.map(one_block, (query_blocks, key_index)).reshape(-1, D)
    return jnp.dot(attended, out_weight, preferred_element_type=jnp.float32).astype(jnp.bfloat16)
```

```python
import functools

import jax
import jax.numpy as jnp
from jax import lax
from jax.experimental import pallas as pl
from jax.experimental.pallas import tpu as pltpu
from jax.sharding import PartitionSpec as P

D = 1024
HEADS = 16
HD = 64
BS = 64
DEG = 8
NEXP = 4
REACH = 2
NL = 3
MESH = pl.DeviceIdType.MESH
F32, BF16 = jnp.float32, jnp.bfloat16
VMEM_LIMIT = 56 * 1024 * 1024


def split(x):
    hi = x.astype(BF16)
    lo = (x - hi.astype(F32)).astype(BF16)
    return jnp.concatenate([hi, lo], axis=-1)


def diffuse_kernel(
    n,
    node_ref,
    struct_ref,
    ops_ref,
    lap_ref,
    coef_ref,
    npool_ref,
    epool_ref,
    pool,
    halo,
    terms,
    enc,
    opcat,
    hsend,
    hrecv,
    nsend,
    nrecv,
    esend,
    erecv,
    own_sem,
):
    count = ops_ref.shape[0]
    rows = count * BS
    rim = REACH * BS
    me = lax.axis_index("seq")
    has_left, has_right = me > 0, me < n - 1
    levels = n.bit_length() - 1
    partners = []
    for link in range(NEXP):
        mask = 2 ** (link * (levels - 1) // (NEXP - 1))
        bit = lax.rem(me // mask, 2)
        partners.append(me + mask * (1 - 2 * bit))

    barrier = pltpu.get_barrier_semaphore()
    for peer in partners:
        pl.semaphore_signal(barrier, inc=1, device_id={"seq": peer}, device_id_type=MESH)

    @pl.when(has_left)
    def _():
        pl.semaphore_signal(barrier, inc=1, device_id={"seq": me - 1}, device_id_type=MESH)

    @pl.when(has_right)
    def _():
        pl.semaphore_signal(barrier, inc=1, device_id={"seq": me + 1}, device_id_type=MESH)

    t0 = struct_ref[...]
    terms[0] = t0.reshape(count, BS, -1)
    terms[1] = jnp.zeros_like(terms[1])
    enc[...] = coef_ref[0] * t0.reshape(count, BS, -1)
    pool[0, REACH : REACH + count] = split(t0).reshape(count, BS, -1)
    peers = NEXP + has_left.astype(jnp.int32) + has_right.astype(jnp.int32)
    pl.semaphore_wait(barrier, peers)

    def to_left(src, dst, send, recv):
        return pltpu.make_async_remote_copy(
            src, dst, send, recv, device_id={"seq": me - 1}, device_id_type=MESH
        )

    def to_right(src, dst, send, recv):
        return pltpu.make_async_remote_copy(
            src, dst, send, recv, device_id={"seq": me + 1}, device_id_type=MESH
        )

    def halo_left(k):
        return to_left(
            pool.at[lax.rem(k, 2), pl.ds(REACH, REACH)], halo.at[k, 1], hsend.at[k, 0], hrecv.at[k, 1]
        )

    def halo_right(k):
        return to_right(
            pool.at[lax.rem(k, 2), pl.ds(count, REACH)], halo.at[k, 0], hsend.at[k, 1], hrecv.at[k, 0]
        )

    def start_halo(k):
        @pl.when(has_left)
        def _():
            halo_left(k).start()

        @pl.when(has_right)
        def _():
            halo_right(k).start()

    def wait_halo(k):
        @pl.when(has_left)
        def _():
            halo_right(k).wait_recv()
            pool[lax.rem(k, 2), 0:REACH] = halo[k, 0]

        @pl.when(has_right)
        def _():
            halo_left(k).wait_recv()
            pool[lax.rem(k, 2), count + REACH :] = halo[k, 1]

    def wait_halo_sent(k):
        @pl.when(has_left)
        def _():
            halo_left(k).wait_send()

        @pl.when(has_right)
        def _():
            halo_right(k).wait_send()

    start_halo(0)

    def near_left(src, dst, width_rows, send, recv):
        return to_left(src.at[pl.ds(0, rim)], dst.at[pl.ds(rim + width_rows, rim)], send.at[NEXP], recv.at[NEXP])

    def near_right(src, dst, width_rows, send, recv):
        return to_right(
            src.at[pl.ds(width_rows - rim, rim)], dst.at[pl.ds(0, rim)], send.at[NEXP + 1], recv.at[NEXP + 1]
        )

    def far(src, dst, link, send, recv):
        return pltpu.make_async_remote_copy(
            src,
            dst.at[pl.ds(2 * rim + rows + link * rows, rows)],
            send.at[link],
            recv.at[link],
            device_id={"seq": partners[link]},
            device_id_type=MESH,
        )

    def start_pool(src, dst, send, recv):
        for link in reversed(range(NEXP)):
            far(src, dst, link, send, recv).start()

        @pl.when(has_left)
        def _():
            near_left(src, dst, rows, send, recv).start()

        @pl.when(has_right)
        def _():
            near_right(src, dst, rows, send, recv).start()

    def wait_pool(src, dst, send, recv):
        for link in range(NEXP):
            copy = far(src, dst, link, send, recv)
            copy.wait_send()
            copy.wait_recv()

        @pl.when(has_left)
        def _():
            near_left(src, dst, rows, send, recv).wait_send()
            near_right(src, dst, rows, send, recv).wait_recv()

        @pl.when(has_right)
        def _():
            near_right(src, dst, rows, send, recv).wait_send()
            near_left(src, dst, rows, send, recv).wait_recv()

    start_pool(node_ref, npool_ref, nsend, nrecv)
    own_copy = pltpu.make_async_copy(node_ref, npool_ref.at[pl.ds(rim, rows)], own_sem)
    own_copy.start()

    for b in range(count):
        wide = jnp.concatenate([ops_ref[b, j] for j in range(NL)], axis=1)
        hi = wide.astype(BF16)
        opcat[b, 0:BS] = hi
        opcat[b, BS : 2 * BS] = (wide - hi.astype(F32)).astype(BF16)

    first = me * count - REACH

    def step(k, carry):
        now, before = lax.rem(k, 2), lax.rem(k + 1, 2)
        factor = jnp.where(k == 1, 1.0, 2.0).astype(F32)

        def block(b):
            picked = jnp.concatenate(
                [pool[before, jnp.clip(lap_ref[b, j] - first, 0, count + 2 * REACH - 1)] for j in range(NL)],
                axis=0,
            )
            r = jnp.dot(opcat[b], picked, preferred_element_type=F32)
            r = r[:BS] + r[BS:]
            r = r[:, : r.shape[1] // 2] + r[:, r.shape[1] // 2 :]
            new = factor * r - terms[now, b]
            terms[now, b] = new
            enc[b] = enc[b] + coef_ref[k] * new
            pool[now, REACH + b] = split(new)

        wait_halo(k - 1)

        @pl.when(k >= 2)
        def _():
            wait_halo_sent(k - 2)

        for b in [*range(REACH), *range(count - REACH, count)]:
            block(b)

        @pl.when(k < DEG)
        def _():
            start_halo(k)

        for b in range(REACH, count - REACH):
            block(b)
        return carry

    lax.fori_loop(1, DEG + 1, step, 0)
    wait_halo_sent(DEG - 1)

    epool_ref[pl.ds(rim, rows)] = enc[...].reshape(rows, -1).astype(BF16)
    own_enc = epool_ref.at[pl.ds(rim, rows)]
    start_pool(own_enc, epool_ref, esend, erecv)
    wait_pool(own_enc, epool_ref, esend, erecv)
    wait_pool(node_ref, npool_ref, nsend, nrecv)
    own_copy.wait()


def attend_kernel(count, slots_ref, npool_ref, epool_ref, we_ref, wqkv_ref, wo_ref, out_ref, blended, kv, qs, att):
    rim = REACH * BS
    chunk = 256
    total = npool_ref.shape[0] // chunk

    def project(c, carry):
        at = pl.ds(pl.multiple_of(c * chunk, chunk), chunk)
        x = jnp.dot(epool_ref[at], we_ref[...], preferred_element_type=F32)
        x = (npool_ref[at].astype(F32) + x).astype(BF16)
        blended[at] = x
        for t in range(4):
            cols = pl.ds(D + t * 512, 512)
            y = jnp.dot(x, wqkv_ref[:, cols], preferred_element_type=F32).astype(BF16)
            kv[pl.ds(c * (chunk // BS), chunk // BS), :, t * 512 : (t + 1) * 512] = y.reshape(chunk // BS, BS, 512)
        return carry

    lax.fori_loop(0, total, project, 0)

    def queries(c, carry):
        at = pl.ds(pl.multiple_of(c * chunk, chunk), chunk)
        x = blended[pl.ds(pl.multiple_of(rim + c * chunk, 128), chunk)]
        for t in range(2):
            cols = pl.ds(t * 512, 512)
            y = jnp.dot(x, wqkv_ref[:, cols], preferred_element_type=F32).astype(BF16)
            qs[at, t * 512 : (t + 1) * 512] = y * jnp.array(1.0 / HD**0.5, BF16)
        return carry

    lax.fori_loop(0, count * BS // chunk, queries, 0)

    pack = 4
    width = pack * HD
    head = lax.broadcasted_iota(jnp.int32, (BS, width), 1) // HD
    keep = [head == h for h in range(pack)]

    def attend(b, carry):
        at = pl.ds(pl.multiple_of(b * BS, BS), BS)
        where = [slots_ref[b, j] for j in range(1 + NL + NEXP)]
        for g in range(HEADS // pack):
            cols = slice(g * width, (g + 1) * width)
            vcols = slice(D + g * width, D + (g + 1) * width)
            q = qs[at, cols]
            q = jnp.concatenate([jnp.where(m, q, jnp.zeros_like(q)) for m in keep], axis=0)
            k = jnp.concatenate([kv[w, :, cols] for w in where], axis=0)
            v = jnp.concatenate([kv[w, :, vcols] for w in where], axis=0)
            s = lax.dot_general(q, k, (((1,), (1,)), ((), ())), preferred_element_type=F32)
            p = jnp.exp(s - jnp.max(s, axis=1, keepdims=True))
            p = (p * (1.0 / jnp.sum(p, axis=1, keepdims=True))).astype(BF16)
            o = jnp.dot(p, v, preferred_element_type=F32)
            mine = o[0:BS]
            for h in range(1, pack):
                mine = jnp.where(keep[h], o[h * BS : (h + 1) * BS], mine)
            att[at, cols] = mine.astype(BF16)
        return carry

    lax.fori_loop(0, count, attend, 0)

    def output(c, carry):
        at = pl.ds(pl.multiple_of(c * chunk, chunk), chunk)
        x = att[at]
        for t in range(2):
            cols = slice(t * 512, (t + 1) * 512)
            out_ref[at, cols] = jnp.dot(x, wo_ref[:, cols], preferred_element_type=F32).astype(BF16)
        return carry

    lax.fori_loop(0, count * BS // chunk, output, 0)


def on_device(
    n,
    node_feats,
    struct_feats,
    op_blocks,
    laplace_index,
    graph_links,
    expander_slot,
    series_coef,
    encode_weight,
    qkv_weight,
    out_weight,
):
    count = op_blocks.shape[0]
    rows, rim, pch = count * BS, REACH * BS, struct_feats.shape[1]
    pool_rows = rows * (1 + NEXP) + 2 * rim
    vmem = pl.BlockSpec(memory_space=pltpu.VMEM)
    smem = pl.BlockSpec(memory_space=pltpu.SMEM)
    hbm = pl.BlockSpec(memory_space=pl.ANY)
    dma = pltpu.SemaphoreType.DMA
    npool, epool = pl.pallas_call(
        functools.partial(diffuse_kernel, n),
        out_shape=(
            jax.ShapeDtypeStruct((pool_rows, D), BF16),
            jax.ShapeDtypeStruct((pool_rows, pch), BF16),
        ),
        in_specs=[hbm, vmem, vmem, smem, smem],
        out_specs=(hbm, vmem),
        scratch_shapes=[
            pltpu.VMEM((2, count + 2 * REACH, BS, 2 * pch), BF16),
            pltpu.VMEM((DEG, 2, REACH, BS, 2 * pch), BF16),
            pltpu.VMEM((2, count, BS, pch), F32),
            pltpu.VMEM((count, BS, pch), F32),
            pltpu.VMEM((count, 2 * BS, NL * BS), BF16),
            dma((DEG, 2)),
            dma((DEG, 2)),
            dma((NEXP + 2,)),
            dma((NEXP + 2,)),
            dma((NEXP + 2,)),
            dma((NEXP + 2,)),
            dma,
        ],
        compiler_params=pltpu.CompilerParams(
            collective_id=0, has_side_effects=True, vmem_limit_bytes=VMEM_LIMIT
        ),
    )(node_feats, struct_feats, op_blocks, laplace_index, series_coef)

    first_block = lax.axis_index("seq") * count
    own_slot = jnp.arange(count, dtype=jnp.int32)[:, None] + REACH
    graph_slot = graph_links - first_block + REACH
    far_base = count + 2 * REACH + jnp.arange(NEXP, dtype=jnp.int32) * count
    slots = jnp.concatenate([own_slot, graph_slot, far_base[None, :] + expander_slot], axis=1)
    return pl.pallas_call(
        functools.partial(attend_kernel, count),
        out_shape=jax.ShapeDtypeStruct((rows, D), BF16),
        in_specs=[smem, vmem, vmem, vmem, vmem, vmem],
        out_specs=vmem,
        scratch_shapes=[
            pltpu.VMEM((pool_rows, D), BF16),
            pltpu.VMEM((pool_rows // BS, BS, 2 * D), BF16),
            pltpu.VMEM((rows, D), BF16),
            pltpu.VMEM((rows, D), BF16),
        ],
        compiler_params=pltpu.CompilerParams(vmem_limit_bytes=VMEM_LIMIT),
    )(slots, npool, epool, encode_weight, qkv_weight, out_weight)


def solution(mesh):
    placed = (
        P(("group", "seq"), None),
        P(("group", "seq"), None),
        P(("group", "seq"), None, None, None),
        P(("group", "seq"), None),
        P(("group", "seq"), None),
        P(("group", "seq"), None),
        P(),
        P(),
        P(),
        P(),
    )
    return jax.shard_map(
        functools.partial(on_device, mesh.shape["seq"]),
        mesh=mesh,
        in_specs=placed,
        out_specs=P(("group", "seq"), None),
        check_vma=False,
    )
```

```python
import functools

import jax
import jax.numpy as jnp
from jax import lax
from jax.experimental import pallas as pl
from jax.experimental.pallas import tpu as pltpu
from jax.sharding import PartitionSpec as P

D = 1024
HEADS = 16
HD = 64
BS = 64
DEG = 8
NEXP = 4
REACH = 2
NL = 3
MESH = pl.DeviceIdType.MESH
F32, BF16 = jnp.float32, jnp.bfloat16
VMEM_LIMIT = 56 * 1024 * 1024


def split(x):
    hi = x.astype(BF16)
    lo = (x - hi.astype(F32)).astype(BF16)
    return jnp.concatenate([hi, lo], axis=-1)


def layer_kernel(
    n,
    node_ref,
    struct_ref,
    ops_ref,
    lap_ref,
    slots_ref,
    coef_ref,
    we_hbm,
    wqkv_hbm,
    wo_hbm,
    out_ref,
    pool0,
    pool1,
    halo,
    term0,
    term1,
    enc,
    opcat,
    npool_ref,
    epool_ref,
    we_ref,
    wqkv_ref,
    wo_ref,
    blended,
    kv,
    qs,
    att,
    hsend,
    hrecv,
    nsend,
    nrecv,
    esend,
    erecv,
    own_sem,
):
    count = ops_ref.shape[0]
    rows = count * BS
    rim = REACH * BS
    me = lax.axis_index("seq")
    has_left, has_right = me > 0, me < n - 1
    levels = n.bit_length() - 1
    partners = []
    for link in range(NEXP):
        mask = 2 ** (link * (levels - 1) // (NEXP - 1))
        bit = lax.rem(me // mask, 2)
        partners.append(me + mask * (1 - 2 * bit))

    barrier = pltpu.get_barrier_semaphore()
    for peer in partners:
        pl.semaphore_signal(barrier, inc=1, device_id={"seq": peer}, device_id_type=MESH)

    @pl.when(has_left)
    def _():
        pl.semaphore_signal(barrier, inc=1, device_id={"seq": me - 1}, device_id_type=MESH)

    @pl.when(has_right)
    def _():
        pl.semaphore_signal(barrier, inc=1, device_id={"seq": me + 1}, device_id_type=MESH)

    own_copies = [
        pltpu.make_async_copy(node_ref, npool_ref.at[pl.ds(rim, rows)], own_sem.at[0]),
        pltpu.make_async_copy(we_hbm, we_ref, own_sem.at[1]),
        pltpu.make_async_copy(wqkv_hbm, wqkv_ref, own_sem.at[2]),
        pltpu.make_async_copy(wo_hbm, wo_ref, own_sem.at[3]),
    ]
    t0 = struct_ref[...]
    term0[...] = t0.reshape(count, BS, -1)
    term1[...] = jnp.zeros_like(term1)
    enc[...] = coef_ref[0] * t0.reshape(count, BS, -1)
    pool0[REACH : REACH + count] = split(t0).reshape(count, BS, -1)
    peers = NEXP + has_left.astype(jnp.int32) + has_right.astype(jnp.int32)
    pl.semaphore_wait(barrier, peers)

    def to_left(src, dst, send, recv):
        return pltpu.make_async_remote_copy(
            src, dst, send, recv, device_id={"seq": me - 1}, device_id_type=MESH
        )

    def to_right(src, dst, send, recv):
        return pltpu.make_async_remote_copy(
            src, dst, send, recv, device_id={"seq": me + 1}, device_id_type=MESH
        )

    pools, terms = (pool0, pool1), (term0, term1)

    def halo_left(k, par):
        return to_left(pools[par].at[pl.ds(REACH, REACH)], halo.at[k, 1], hsend.at[k, 0], hrecv.at[k, 1])

    def halo_right(k, par):
        return to_right(pools[par].at[pl.ds(count, REACH)], halo.at[k, 0], hsend.at[k, 1], hrecv.at[k, 0])

    def start_halo(k, par):
        @pl.when(has_left)
        def _():
            halo_left(k, par).start()

        @pl.when(has_right)
        def _():
            halo_right(k, par).start()

    def wait_halo(k, par):
        @pl.when(has_left)
        def _():
            halo_right(k, par).wait_recv()
            pools[par][0:REACH] = halo[k, 0]

        @pl.when(has_right)
        def _():
            halo_left(k, par).wait_recv()
            pools[par][count + REACH :] = halo[k, 1]

    def wait_halo_sent(k, par):
        @pl.when(has_left)
        def _():
            halo_left(k, par).wait_send()

        @pl.when(has_right)
        def _():
            halo_right(k, par).wait_send()

    start_halo(0, 0)

    def near_left(src, dst, width_rows, send, recv):
        return to_left(src.at[pl.ds(0, rim)], dst.at[pl.ds(rim + width_rows, rim)], send.at[NEXP], recv.at[NEXP])

    def near_right(src, dst, width_rows, send, recv):
        return to_right(
            src.at[pl.ds(width_rows - rim, rim)], dst.at[pl.ds(0, rim)], send.at[NEXP + 1], recv.at[NEXP + 1]
        )

    def far(src, dst, link, send, recv, start=0, size=rows):
        return pltpu.make_async_remote_copy(
            src.at[pl.ds(start, size)],
            dst.at[pl.ds(2 * rim + rows + link * rows + start, size)],
            send.at[link],
            recv.at[link],
            device_id={"seq": partners[link]},
            device_id_type=MESH,
        )

    def start_near(src, dst, send, recv):
        @pl.when(has_left)
        def _():
            near_left(src, dst, rows, send, recv).start()

        @pl.when(has_right)
        def _():
            near_right(src, dst, rows, send, recv).start()

    def wait_near(src, dst, send, recv):
        @pl.when(has_left)
        def _():
            near_left(src, dst, rows, send, recv).wait_send()
            near_right(src, dst, rows, send, recv).wait_recv()

        @pl.when(has_right)
        def _():
            near_right(src, dst, rows, send, recv).wait_send()
            near_left(src, dst, rows, send, recv).wait_recv()

    piece = rows // DEG

    def start_piece(k):
        for link in reversed(range(NEXP)):
            far(node_ref, npool_ref, link, nsend, nrecv, pl.multiple_of(k * piece, piece), piece).start()

    for copy in own_copies:
        copy.start()

    for b in range(count):
        wide = jnp.concatenate([ops_ref[b, j] for j in range(NL)], axis=1)
        hi = wide.astype(BF16)
        opcat[b, 0:BS] = hi
        opcat[b, BS : 2 * BS] = (wide - hi.astype(F32)).astype(BF16)

    first = me * count - REACH

    def group(blocks, k, par, factor):
        src, dst, term = pools[1 - par], pools[par], terms[par]
        news = []
        for b in blocks:
            picked = jnp.concatenate(
                [src[jnp.clip(lap_ref[b, j] - first, 0, count + 2 * REACH - 1)] for j in range(NL)], axis=0
            )
            r = jnp.dot(opcat[b], picked, preferred_element_type=F32)
            r = r[:BS] + r[BS:]
            r = r[:, : r.shape[1] // 2] + r[:, r.shape[1] // 2 :]
            news.append(factor * r - term[b])
        sums = [enc[b] + coef_ref[k] * new for b, new in zip(blocks, news)]
        for b, new, total in zip(blocks, news, sums):
            dst[REACH + b] = split(new)
            term[b] = new
            enc[b] = total

    edges = [*range(REACH), *range(count - REACH, count)]
    inner = list(range(REACH, count - REACH))

    def two_steps(i, carry):
        k = 2 * i + 1
        wait_halo(k - 1, 0)

        @pl.when(i > 0)
        def _():
            wait_halo_sent(k - 2, 1)

        factor = jnp.where(i == 0, 1.0, 2.0).astype(F32)
        group(edges, k, 1, factor)
        start_halo(k, 1)
        start_piece(k - 1)
        group(inner, k, 1, factor)
        k = 2 * i + 2
        wait_halo(k - 1, 1)
        wait_halo_sent(k - 2, 0)
        group(edges, k, 0, 2.0)

        @pl.when(k < DEG)
        def _():
            start_halo(k, 0)

        start_piece(k - 1)
        group(inner, k, 0, 2.0)
        return carry

    lax.fori_loop(0, DEG // 2, two_steps, 0)
    wait_halo_sent(DEG - 1, 1)

    epool_ref[pl.ds(rim, rows)] = enc[...].reshape(rows, -1).astype(BF16)
    own_enc = epool_ref.at[pl.ds(rim, rows)]
    start_near(own_enc, epool_ref, esend, erecv)
    for link in range(NEXP):
        far(own_enc, epool_ref, link, esend, erecv).start()
    start_near(node_ref, npool_ref, nsend, nrecv)
    for copy in own_copies:
        copy.wait()

    tile = 512

    def blend(at, size):
        x = jnp.dot(epool_ref[at], we_ref[...], preferred_element_type=F32)
        blended[0:size] = (npool_ref[at].astype(F32) + x).astype(BF16)

    def keys_values(row, size):
        def columns(t, carry):
            cols = pl.ds(pl.multiple_of(D + t * tile, tile), tile)
            y = jnp.dot(blended[0:size], wqkv_ref[:, cols], preferred_element_type=F32).astype(BF16)
            to = pl.ds(pl.multiple_of(t * tile, tile), tile)
            kv[row // BS : (row + size) // BS, :, to] = y.reshape(size // BS, BS, tile)
            return carry

        lax.fori_loop(0, 2 * D // tile, columns, 0)

    blend(pl.ds(rim, rows), rows)

    def queries(t, carry):
        cols = pl.ds(pl.multiple_of(t * tile, tile), tile)
        y = jnp.dot(blended[0:rows], wqkv_ref[:, cols], preferred_element_type=F32).astype(BF16)
        qs[:, cols] = y * jnp.array(1.0 / HD**0.5, BF16)
        return carry

    lax.fori_loop(0, D // tile, queries, 0)
    keys_values(rim, rows)
    for link in range(NEXP):
        for src, dst, send, recv in ((own_enc, epool_ref, esend, erecv), (node_ref, npool_ref, nsend, nrecv)):
            copy = far(src, dst, link, send, recv)
            copy.wait_send()
            copy.wait_recv()
        row = 2 * rim + rows + link * rows
        blend(pl.ds(row, rows), rows)
        keys_values(row, rows)
        if link == 0:
            wait_near(own_enc, epool_ref, esend, erecv)
            wait_near(node_ref, npool_ref, nsend, nrecv)
            for row in (0, rim + rows):
                blend(pl.ds(row, rim), rim)
                keys_values(row, rim)

    pack = 4
    width = pack * HD
    head = lax.broadcasted_iota(jnp.int32, (BS, width), 1) // HD
    keep = [head == h for h in range(pack)]

    def attend(b, carry):
        at = pl.ds(pl.multiple_of(b * BS, BS), BS)
        where = [slots_ref[b, j] for j in range(1 + NL + NEXP)]
        results = []
        for g in range(HEADS // pack):
            cols = slice(g * width, (g + 1) * width)
            vcols = slice(D + g * width, D + (g + 1) * width)
            q = qs[at, cols]
            q = jnp.concatenate([jnp.where(m, q, jnp.zeros_like(q)) for m in keep], axis=0)
            k = jnp.concatenate([kv[w, :, cols] for w in where], axis=0)
            v = jnp.concatenate([kv[w, :, vcols] for w in where], axis=0)
            s = lax.dot_general(q, k, (((1,), (1,)), ((), ())), preferred_element_type=F32)
            p = jnp.exp(s - jnp.max(s, axis=1, keepdims=True))
            p = (p * (1.0 / jnp.sum(p, axis=1, keepdims=True))).astype(BF16)
            o = jnp.dot(p, v, preferred_element_type=F32)
            mine = o[0:BS]
            for h in range(1, pack):
                mine = jnp.where(keep[h], o[h * BS : (h + 1) * BS], mine)
            results.append(mine.astype(BF16))
        for g, result in enumerate(results):
            att[at, g * width : (g + 1) * width] = result
        return carry

    lax.fori_loop(0, count, attend, 0)

    def output(t, carry):
        cols = pl.ds(pl.multiple_of(t * tile, tile), tile)
        out_ref[:, cols] = jnp.dot(att[...], wo_ref[:, cols], preferred_element_type=F32).astype(BF16)
        return carry

    lax.fori_loop(0, D // tile, output, 0)


def on_device(
    n,
    node_feats,
    struct_feats,
    op_blocks,
    laplace_index,
    graph_links,
    expander_slot,
    series_coef,
    encode_weight,
    qkv_weight,
    out_weight,
):
    count = op_blocks.shape[0]
    rows, rim, pch = count * BS, REACH * BS, struct_feats.shape[1]
    pool_rows = rows * (1 + NEXP) + 2 * rim
    vmem = pl.BlockSpec(memory_space=pltpu.VMEM)
    smem = pl.BlockSpec(memory_space=pltpu.SMEM)
    hbm = pl.BlockSpec(memory_space=pl.ANY)
    dma = pltpu.SemaphoreType.DMA
    first_block = lax.axis_index("seq") * count
    own_slot = jnp.arange(count, dtype=jnp.int32)[:, None] + REACH
    graph_slot = graph_links - first_block + REACH
    far_base = count + 2 * REACH + jnp.arange(NEXP, dtype=jnp.int32) * count
    slots = jnp.concatenate([own_slot, graph_slot, far_base[None, :] + expander_slot], axis=1)
    return pl.pallas_call(
        functools.partial(layer_kernel, n),
        out_shape=jax.ShapeDtypeStruct((rows, D), BF16),
        in_specs=[hbm, vmem, vmem, smem, smem, smem, hbm, hbm, hbm],
        out_specs=vmem,
        scratch_shapes=[
            pltpu.VMEM((count + 2 * REACH, BS, 2 * pch), BF16),
            pltpu.VMEM((count + 2 * REACH, BS, 2 * pch), BF16),
            pltpu.VMEM((DEG, 2, REACH, BS, 2 * pch), BF16),
            pltpu.VMEM((count, BS, pch), F32),
            pltpu.VMEM((count, BS, pch), F32),
            pltpu.VMEM((count, BS, pch), F32),
            pltpu.VMEM((count, 2 * BS, NL * BS), BF16),
            pltpu.VMEM((pool_rows, D), BF16),
            pltpu.VMEM((pool_rows, pch), BF16),
            pltpu.VMEM(encode_weight.shape, BF16),
            pltpu.VMEM(qkv_weight.shape, BF16),
            pltpu.VMEM(out_weight.shape, BF16),
            pltpu.VMEM((rows, D), BF16),
            pltpu.VMEM((pool_rows // BS, BS, 2 * D), BF16),
            pltpu.VMEM((rows, D), BF16),
            pltpu.VMEM((rows, D), BF16),
            dma((DEG, 2)),
            dma((DEG, 2)),
            dma((NEXP + 2,)),
            dma((NEXP + 2,)),
            dma((NEXP + 2,)),
            dma((NEXP + 2,)),
            dma((4,)),
        ],
        compiler_params=pltpu.CompilerParams(
            collective_id=0, has_side_effects=True, vmem_limit_bytes=VMEM_LIMIT
        ),
    )(
        node_feats,
        struct_feats,
        op_blocks,
        laplace_index,
        slots,
        series_coef,
        encode_weight,
        qkv_weight,
        out_weight,
    )


def solution(mesh):
    placed = (
        P(("group", "seq"), None),
        P(("group", "seq"), None),
        P(("group", "seq"), None, None, None),
        P(("group", "seq"), None),
        P(("group", "seq"), None),
        P(("group", "seq"), None),
        P(),
        P(),
        P(),
        P(),
    )
    return jax.shard_map(
        functools.partial(on_device, mesh.shape["seq"]),
        mesh=mesh,
        in_specs=placed,
        out_specs=P(("group", "seq"), None),
        check_vma=False,
    )
```

```python
import functools

import jax
import jax.numpy as jnp
from jax import lax
from jax.experimental import pallas as pl
from jax.experimental.pallas import tpu as pltpu
from jax.sharding import PartitionSpec as P

D = 1024
HEADS = 16
HD = 64
BS = 64
DEG = 8
NEXP = 4
REACH = 2
NL = 3
MESH = pl.DeviceIdType.MESH
F32, BF16 = jnp.float32, jnp.bfloat16
VMEM_LIMIT = 56 * 1024 * 1024


def split(x):
    hi = x.astype(BF16)
    lo = (x - hi.astype(F32)).astype(BF16)
    return jnp.concatenate([hi, lo], axis=-1)


def layer_kernel(
    n,
    node_ref,
    struct_ref,
    ops_ref,
    lap_ref,
    slots_ref,
    coef_ref,
    we_hbm,
    wqkv_hbm,
    wo_hbm,
    out_ref,
    pool0,
    pool1,
    halo,
    term0,
    term1,
    enc,
    opcat,
    npool_ref,
    epool_ref,
    we_ref,
    wqkv_ref,
    wo_ref,
    blended,
    kv,
    qs,
    att,
    hsend,
    hrecv,
    nsend,
    nrecv,
    esend,
    erecv,
    own_sem,
):
    count = ops_ref.shape[0]
    rows = count * BS
    rim = REACH * BS
    me = lax.axis_index("seq")
    has_left, has_right = me > 0, me < n - 1
    levels = n.bit_length() - 1
    partners = []
    for link in range(NEXP):
        mask = 2 ** (link * (levels - 1) // (NEXP - 1))
        bit = lax.rem(me // mask, 2)
        partners.append(me + mask * (1 - 2 * bit))

    barrier = pltpu.get_barrier_semaphore()
    for peer in partners:
        pl.semaphore_signal(barrier, inc=1, device_id={"seq": peer}, device_id_type=MESH)

    @pl.when(has_left)
    def _():
        pl.semaphore_signal(barrier, inc=1, device_id={"seq": me - 1}, device_id_type=MESH)

    @pl.when(has_right)
    def _():
        pl.semaphore_signal(barrier, inc=1, device_id={"seq": me + 1}, device_id_type=MESH)

    own_copies = [
        pltpu.make_async_copy(node_ref, npool_ref.at[pl.ds(rim, rows)], own_sem.at[0]),
        pltpu.make_async_copy(we_hbm, we_ref, own_sem.at[1]),
        pltpu.make_async_copy(wqkv_hbm, wqkv_ref, own_sem.at[2]),
        pltpu.make_async_copy(wo_hbm, wo_ref, own_sem.at[3]),
    ]
    t0 = struct_ref[...]
    term0[...] = t0.reshape(count, BS, -1)
    term1[...] = jnp.zeros_like(term1)
    enc[...] = coef_ref[0] * t0.reshape(count, BS, -1)
    pool0[REACH : REACH + count] = split(t0).reshape(count, BS, -1)
    peers = NEXP + has_left.astype(jnp.int32) + has_right.astype(jnp.int32)
    pl.semaphore_wait(barrier, peers)

    def to_left(src, dst, send, recv):
        return pltpu.make_async_remote_copy(
            src, dst, send, recv, device_id={"seq": me - 1}, device_id_type=MESH
        )

    def to_right(src, dst, send, recv):
        return pltpu.make_async_remote_copy(
            src, dst, send, recv, device_id={"seq": me + 1}, device_id_type=MESH
        )

    pools, terms = (pool0, pool1), (term0, term1)

    def halo_left(k, par):
        return to_left(pools[par].at[pl.ds(REACH, REACH)], halo.at[k, 1], hsend.at[k, 0], hrecv.at[k, 1])

    def halo_right(k, par):
        return to_right(pools[par].at[pl.ds(count, REACH)], halo.at[k, 0], hsend.at[k, 1], hrecv.at[k, 0])

    def start_halo(k, par):
        @pl.when(has_left)
        def _():
            halo_left(k, par).start()

        @pl.when(has_right)
        def _():
            halo_right(k, par).start()

    def wait_halo(k, par):
        @pl.when(has_left)
        def _():
            halo_right(k, par).wait_recv()
            pools[par][0:REACH] = halo[k, 0]

        @pl.when(has_right)
        def _():
            halo_left(k, par).wait_recv()
            pools[par][count + REACH :] = halo[k, 1]

    def wait_halo_sent(k, par):
        @pl.when(has_left)
        def _():
            halo_left(k, par).wait_send()

        @pl.when(has_right)
        def _():
            halo_right(k, par).wait_send()

    start_halo(0, 0)

    def near_left(src, dst, width_rows, send, recv):
        return to_left(src.at[pl.ds(0, rim)], dst.at[pl.ds(rim + width_rows, rim)], send.at[NEXP], recv.at[NEXP])

    def near_right(src, dst, width_rows, send, recv):
        return to_right(
            src.at[pl.ds(width_rows - rim, rim)], dst.at[pl.ds(0, rim)], send.at[NEXP + 1], recv.at[NEXP + 1]
        )

    def far(src, dst, link, send, recv, start=0, size=rows):
        return pltpu.make_async_remote_copy(
            src.at[pl.ds(start, size)],
            dst.at[pl.ds(2 * rim + rows + link * rows + start, size)],
            send.at[link],
            recv.at[link],
            device_id={"seq": partners[link]},
            device_id_type=MESH,
        )

    def start_near(src, dst, send, recv):
        @pl.when(has_left)
        def _():
            near_left(src, dst, rows, send, recv).start()

        @pl.when(has_right)
        def _():
            near_right(src, dst, rows, send, recv).start()

    def wait_near(src, dst, send, recv):
        @pl.when(has_left)
        def _():
            near_left(src, dst, rows, send, recv).wait_send()
            near_right(src, dst, rows, send, recv).wait_recv()

        @pl.when(has_right)
        def _():
            near_right(src, dst, rows, send, recv).wait_send()
            near_left(src, dst, rows, send, recv).wait_recv()

    sizes = [rows // DEG if link < NEXP // 2 else rows // DEG * 3 // 4 for link in range(NEXP)]

    def start_piece(k):
        for link in reversed(range(NEXP)):
            at = k * sizes[link]
            if not isinstance(k, int):
                at = pl.multiple_of(at, 16)
            far(node_ref, npool_ref, link, nsend, nrecv, at, sizes[link]).start()

    def start_rest():
        for link in range(NEXP):
            sent = DEG * sizes[link]
            if sent < rows:
                far(node_ref, npool_ref, link, nsend, nrecv, sent, rows - sent).start()

    start_piece(0)
    for copy in own_copies:
        copy.start()

    for b in range(count):
        wide = jnp.concatenate([ops_ref[b, j] for j in range(NL)], axis=1)
        hi = wide.astype(BF16)
        opcat[b, 0:BS] = hi
        opcat[b, BS : 2 * BS] = (wide - hi.astype(F32)).astype(BF16)

    first = me * count - REACH

    def group(blocks, k, par, factor):
        src, dst, term = pools[1 - par], pools[par], terms[par]
        news = []
        for b in blocks:
            picked = jnp.concatenate(
                [src[jnp.clip(lap_ref[b, j] - first, 0, count + 2 * REACH - 1)] for j in range(NL)], axis=0
            )
            r = jnp.dot(opcat[b], picked, preferred_element_type=F32)
            r = r[:BS] + r[BS:]
            r = r[:, : r.shape[1] // 2] + r[:, r.shape[1] // 2 :]
            news.append(factor * r - term[b])
        sums = [enc[b] + coef_ref[k] * new for b, new in zip(blocks, news)]
        for b, new, total in zip(blocks, news, sums):
            dst[REACH + b] = split(new)
            term[b] = new
            enc[b] = total

    edges = [*range(REACH), *range(count - REACH, count)]
    inner = list(range(REACH, count - REACH))

    def two_steps(i, carry):
        k = 2 * i + 1
        wait_halo(k - 1, 0)

        @pl.when(i > 0)
        def _():
            wait_halo_sent(k - 2, 1)

        factor = jnp.where(i == 0, 1.0, 2.0).astype(F32)
        group(edges, k, 1, factor)
        start_halo(k, 1)
        start_piece(k)
        group(inner, k, 1, factor)
        k = 2 * i + 2
        wait_halo(k - 1, 1)
        wait_halo_sent(k - 2, 0)
        group(edges, k, 0, 2.0)

        @pl.when(k < DEG)
        def _():
            start_halo(k, 0)
            start_piece(k)

        group(inner, k, 0, 2.0)
        return carry

    lax.fori_loop(0, DEG // 2, two_steps, 0)
    wait_halo_sent(DEG - 1, 1)

    epool_ref[pl.ds(rim, rows)] = enc[...].reshape(rows, -1).astype(BF16)
    own_enc = epool_ref.at[pl.ds(rim, rows)]
    start_near(own_enc, epool_ref, esend, erecv)
    for link in range(NEXP):
        far(own_enc, epool_ref, link, esend, erecv).start()
    start_near(node_ref, npool_ref, nsend, nrecv)
    start_rest()
    for copy in own_copies:
        copy.wait()

    tile = 512

    def blend(at, size):
        x = jnp.dot(epool_ref[at], we_ref[...], preferred_element_type=F32)
        blended[0:size] = (npool_ref[at].astype(F32) + x).astype(BF16)

    def keys_values(row, size):
        def columns(t, carry):
            cols = pl.ds(pl.multiple_of(D + t * tile, tile), tile)
            y = jnp.dot(blended[0:size], wqkv_ref[:, cols], preferred_element_type=F32).astype(BF16)
            to = pl.ds(pl.multiple_of(t * tile, tile), tile)
            kv[row // BS : (row + size) // BS, :, to] = y.reshape(size // BS, BS, tile)
            return carry

        lax.fori_loop(0, 2 * D // tile, columns, 0)

    blend(pl.ds(rim, rows), rows)

    def queries(t, carry):
        cols = pl.ds(pl.multiple_of(t * tile, tile), tile)
        y = jnp.dot(blended[0:rows], wqkv_ref[:, cols], preferred_element_type=F32).astype(BF16)
        qs[:, cols] = y * jnp.array(1.0 / HD**0.5, BF16)
        return carry

    lax.fori_loop(0, D // tile, queries, 0)
    keys_values(rim, rows)
    for link in range(NEXP):
        for src, dst, send, recv in ((own_enc, epool_ref, esend, erecv), (node_ref, npool_ref, nsend, nrecv)):
            copy = far(src, dst, link, send, recv)
            copy.wait_send()
            copy.wait_recv()
        row = 2 * rim + rows + link * rows
        blend(pl.ds(row, rows), rows)
        keys_values(row, rows)
        if link == 0:
            wait_near(own_enc, epool_ref, esend, erecv)
            wait_near(node_ref, npool_ref, nsend, nrecv)
            for row in (0, rim + rows):
                blend(pl.ds(row, rim), rim)
                keys_values(row, rim)

    pack = 4
    width = pack * HD
    head = lax.broadcasted_iota(jnp.int32, (BS, width), 1) // HD
    keep = [head == h for h in range(pack)]

    def attend(b, carry):
        at = pl.ds(pl.multiple_of(b * BS, BS), BS)
        where = [slots_ref[b, j] for j in range(1 + NL + NEXP)]
        results = []
        for g in range(HEADS // pack):
            cols = slice(g * width, (g + 1) * width)
            vcols = slice(D + g * width, D + (g + 1) * width)
            q = qs[at, cols]
            q = jnp.concatenate([jnp.where(m, q, jnp.zeros_like(q)) for m in keep], axis=0)
            k = jnp.concatenate([kv[w, :, cols] for w in where], axis=0)
            v = jnp.concatenate([kv[w, :, vcols] for w in where], axis=0)
            s = lax.dot_general(q, k, (((1,), (1,)), ((), ())), preferred_element_type=F32)
            p = jnp.exp(s - jnp.max(s, axis=1, keepdims=True))
            p = (p * (1.0 / jnp.sum(p, axis=1, keepdims=True))).astype(BF16)
            o = jnp.dot(p, v, preferred_element_type=F32)
            mine = o[0:BS]
            for h in range(1, pack):
                mine = jnp.where(keep[h], o[h * BS : (h + 1) * BS], mine)
            results.append(mine.astype(BF16))
        for g, result in enumerate(results):
            att[at, g * width : (g + 1) * width] = result
        return carry

    lax.fori_loop(0, count, attend, 0)

    def output(t, carry):
        cols = pl.ds(pl.multiple_of(t * tile, tile), tile)
        out_ref[:, cols] = jnp.dot(att[...], wo_ref[:, cols], preferred_element_type=F32).astype(BF16)
        return carry

    lax.fori_loop(0, D // tile, output, 0)


def on_device(
    n,
    node_feats,
    struct_feats,
    op_blocks,
    laplace_index,
    graph_links,
    expander_slot,
    series_coef,
    encode_weight,
    qkv_weight,
    out_weight,
):
    count = op_blocks.shape[0]
    rows, rim, pch = count * BS, REACH * BS, struct_feats.shape[1]
    pool_rows = rows * (1 + NEXP) + 2 * rim
    vmem = pl.BlockSpec(memory_space=pltpu.VMEM)
    smem = pl.BlockSpec(memory_space=pltpu.SMEM)
    hbm = pl.BlockSpec(memory_space=pl.ANY)
    dma = pltpu.SemaphoreType.DMA
    first_block = lax.axis_index("seq") * count
    own_slot = jnp.arange(count, dtype=jnp.int32)[:, None] + REACH
    graph_slot = graph_links - first_block + REACH
    far_base = count + 2 * REACH + jnp.arange(NEXP, dtype=jnp.int32) * count
    slots = jnp.concatenate([own_slot, graph_slot, far_base[None, :] + expander_slot], axis=1)
    return pl.pallas_call(
        functools.partial(layer_kernel, n),
        out_shape=jax.ShapeDtypeStruct((rows, D), BF16),
        in_specs=[hbm, vmem, vmem, smem, smem, smem, hbm, hbm, hbm],
        out_specs=vmem,
        scratch_shapes=[
            pltpu.VMEM((count + 2 * REACH, BS, 2 * pch), BF16),
            pltpu.VMEM((count + 2 * REACH, BS, 2 * pch), BF16),
            pltpu.VMEM((DEG, 2, REACH, BS, 2 * pch), BF16),
            pltpu.VMEM((count, BS, pch), F32),
            pltpu.VMEM((count, BS, pch), F32),
            pltpu.VMEM((count, BS, pch), F32),
            pltpu.VMEM((count, 2 * BS, NL * BS), BF16),
            pltpu.VMEM((pool_rows, D), BF16),
            pltpu.VMEM((pool_rows, pch), BF16),
            pltpu.VMEM(encode_weight.shape, BF16),
            pltpu.VMEM(qkv_weight.shape, BF16),
            pltpu.VMEM(out_weight.shape, BF16),
            pltpu.VMEM((rows, D), BF16),
            pltpu.VMEM((pool_rows // BS, BS, 2 * D), BF16),
            pltpu.VMEM((rows, D), BF16),
            pltpu.VMEM((rows, D), BF16),
            dma((DEG, 2)),
            dma((DEG, 2)),
            dma((NEXP + 2,)),
            dma((NEXP + 2,)),
            dma((NEXP + 2,)),
            dma((NEXP + 2,)),
            dma((4,)),
        ],
        compiler_params=pltpu.CompilerParams(
            collective_id=0, has_side_effects=True, vmem_limit_bytes=VMEM_LIMIT
        ),
    )(
        node_feats,
        struct_feats,
        op_blocks,
        laplace_index,
        slots,
        series_coef,
        encode_weight,
        qkv_weight,
        out_weight,
    )


def solution(mesh):
    placed = (
        P(("group", "seq"), None),
        P(("group", "seq"), None),
        P(("group", "seq"), None, None, None),
        P(("group", "seq"), None),
        P(("group", "seq"), None),
        P(("group", "seq"), None),
        P(),
        P(),
        P(),
        P(),
    )
    return jax.shard_map(
        functools.partial(on_device, mesh.shape["seq"]),
        mesh=mesh,
        in_specs=placed,
        out_specs=P(("group", "seq"), None),
        check_vma=False,
    )
```

```python
import functools

import jax
import jax.numpy as jnp
from jax import lax
from jax.experimental import pallas as pl
from jax.experimental.pallas import tpu as pltpu
from jax.sharding import PartitionSpec as P

D = 1024
HEADS = 16
HD = 64
BS = 64
DEG = 8
NEXP = 4
REACH = 2
NL = 3
MESH = pl.DeviceIdType.MESH
F32, BF16 = jnp.float32, jnp.bfloat16
VMEM_LIMIT = 56 * 1024 * 1024


def split(x):
    hi = x.astype(BF16)
    lo = (x - hi.astype(F32)).astype(BF16)
    return jnp.concatenate([hi, lo], axis=-1)


def layer_kernel(
    n,
    node_ref,
    struct_ref,
    ops_ref,
    lap_ref,
    slots_ref,
    coef_ref,
    we_hbm,
    wqkv_hbm,
    wo_hbm,
    out_ref,
    pool0,
    pool1,
    halo,
    term0,
    term1,
    enc,
    opcat,
    npool_ref,
    epool_ref,
    we_ref,
    wqkv_ref,
    wo_ref,
    blended,
    kv,
    qs,
    att,
    hsend,
    hrecv,
    nsend,
    nrecv,
    esend,
    erecv,
    own_sem,
):
    count = ops_ref.shape[0]
    rows = count * BS
    rim = REACH * BS
    me = lax.axis_index("seq")
    has_left, has_right = me > 0, me < n - 1
    levels = n.bit_length() - 1
    partners = []
    for link in range(NEXP):
        mask = 2 ** (link * (levels - 1) // (NEXP - 1))
        bit = lax.rem(me // mask, 2)
        partners.append(me + mask * (1 - 2 * bit))

    barrier = pltpu.get_barrier_semaphore()
    for peer in partners:
        pl.semaphore_signal(barrier, inc=1, device_id={"seq": peer}, device_id_type=MESH)

    @pl.when(has_left)
    def _():
        pl.semaphore_signal(barrier, inc=1, device_id={"seq": me - 1}, device_id_type=MESH)

    @pl.when(has_right)
    def _():
        pl.semaphore_signal(barrier, inc=1, device_id={"seq": me + 1}, device_id_type=MESH)

    own_copies = [
        pltpu.make_async_copy(node_ref, npool_ref.at[pl.ds(rim, rows)], own_sem.at[0]),
        pltpu.make_async_copy(we_hbm, we_ref, own_sem.at[1]),
        pltpu.make_async_copy(wqkv_hbm, wqkv_ref, own_sem.at[2]),
        pltpu.make_async_copy(wo_hbm, wo_ref, own_sem.at[3]),
    ]
    t0 = struct_ref[...]
    term0[...] = t0.reshape(count, BS, -1)
    term1[...] = jnp.zeros_like(term1)
    enc[...] = coef_ref[0] * t0.reshape(count, BS, -1)
    pool0[REACH : REACH + count] = split(t0).reshape(count, BS, -1)
    peers = NEXP + has_left.astype(jnp.int32) + has_right.astype(jnp.int32)
    pl.semaphore_wait(barrier, peers)

    def to_left(src, dst, send, recv):
        return pltpu.make_async_remote_copy(
            src, dst, send, recv, device_id={"seq": me - 1}, device_id_type=MESH
        )

    def to_right(src, dst, send, recv):
        return pltpu.make_async_remote_copy(
            src, dst, send, recv, device_id={"seq": me + 1}, device_id_type=MESH
        )

    pools, terms = (pool0, pool1), (term0, term1)

    def halo_left(k, par):
        return to_left(pools[par].at[pl.ds(REACH, REACH)], halo.at[k, 1], hsend.at[k, 0], hrecv.at[k, 1])

    def halo_right(k, par):
        return to_right(pools[par].at[pl.ds(count, REACH)], halo.at[k, 0], hsend.at[k, 1], hrecv.at[k, 0])

    def start_halo(k, par):
        @pl.when(has_left)
        def _():
            halo_left(k, par).start()

        @pl.when(has_right)
        def _():
            halo_right(k, par).start()

    def wait_halo(k, par):
        @pl.when(has_left)
        def _():
            halo_right(k, par).wait_recv()
            pools[par][0:REACH] = halo[k, 0]

        @pl.when(has_right)
        def _():
            halo_left(k, par).wait_recv()
            pools[par][count + REACH :] = halo[k, 1]

    def wait_halo_sent(k, par):
        @pl.when(has_left)
        def _():
            halo_left(k, par).wait_send()

        @pl.when(has_right)
        def _():
            halo_right(k, par).wait_send()

    start_halo(0, 0)

    def near_left(src, dst, width_rows, send, recv):
        return to_left(src.at[pl.ds(0, rim)], dst.at[pl.ds(rim + width_rows, rim)], send.at[NEXP], recv.at[NEXP])

    def near_right(src, dst, width_rows, send, recv):
        return to_right(
            src.at[pl.ds(width_rows - rim, rim)], dst.at[pl.ds(0, rim)], send.at[NEXP + 1], recv.at[NEXP + 1]
        )

    def far(src, dst, link, send, recv, start=0, size=rows):
        return pltpu.make_async_remote_copy(
            src.at[pl.ds(start, size)],
            dst.at[pl.ds(2 * rim + rows + link * rows + start, size)],
            send.at[link],
            recv.at[link],
            device_id={"seq": partners[link]},
            device_id_type=MESH,
        )

    def start_near(src, dst, send, recv):
        @pl.when(has_left)
        def _():
            near_left(src, dst, rows, send, recv).start()

        @pl.when(has_right)
        def _():
            near_right(src, dst, rows, send, recv).start()

    def wait_near(src, dst, send, recv):
        @pl.when(has_left)
        def _():
            near_left(src, dst, rows, send, recv).wait_send()
            near_right(src, dst, rows, send, recv).wait_recv()

        @pl.when(has_right)
        def _():
            near_right(src, dst, rows, send, recv).wait_send()
            near_left(src, dst, rows, send, recv).wait_recv()

    sizes = [rows // DEG if link < NEXP // 2 else rows // DEG // 2 for link in range(NEXP)]

    def start_piece(k):
        for link in reversed(range(NEXP)):
            at = k * sizes[link]
            if not isinstance(k, int):
                at = pl.multiple_of(at, 16)
            far(node_ref, npool_ref, link, nsend, nrecv, at, sizes[link]).start()

    def start_rest():
        for link in range(NEXP):
            sent = DEG * sizes[link]
            if sent < rows:
                far(node_ref, npool_ref, link, nsend, nrecv, sent, rows - sent).start()

    start_piece(0)
    for copy in own_copies:
        copy.start()

    for b in range(count):
        wide = jnp.concatenate([ops_ref[b, j] for j in range(NL)], axis=1)
        hi = wide.astype(BF16)
        opcat[b, 0:BS] = hi
        opcat[b, BS : 2 * BS] = (wide - hi.astype(F32)).astype(BF16)

    first = me * count - REACH

    def group(blocks, k, par, factor):
        src, dst, term = pools[1 - par], pools[par], terms[par]
        news = []
        for b in blocks:
            picked = jnp.concatenate(
                [src[jnp.clip(lap_ref[b, j] - first, 0, count + 2 * REACH - 1)] for j in range(NL)], axis=0
            )
            r = jnp.dot(opcat[b], picked, preferred_element_type=F32)
            r = r[:BS] + r[BS:]
            r = r[:, : r.shape[1] // 2] + r[:, r.shape[1] // 2 :]
            news.append(factor * r - term[b])
        sums = [enc[b] + coef_ref[k] * new for b, new in zip(blocks, news)]
        for b, new, total in zip(blocks, news, sums):
            dst[REACH + b] = split(new)
            term[b] = new
            enc[b] = total

    edges = [*range(REACH), *range(count - REACH, count)]
    inner = list(range(REACH, count - REACH))

    def two_steps(i, carry):
        k = 2 * i + 1
        wait_halo(k - 1, 0)

        @pl.when(i > 0)
        def _():
            wait_halo_sent(k - 2, 1)

        factor = jnp.where(i == 0, 1.0, 2.0).astype(F32)
        group(edges, k, 1, factor)
        start_halo(k, 1)
        start_piece(k)
        group(inner, k, 1, factor)
        k = 2 * i + 2
        wait_halo(k - 1, 1)
        wait_halo_sent(k - 2, 0)
        group(edges, k, 0, 2.0)

        @pl.when(k < DEG)
        def _():
            start_halo(k, 0)
            start_piece(k)

        group(inner, k, 0, 2.0)
        return carry

    lax.fori_loop(0, DEG // 2, two_steps, 0)
    wait_halo_sent(DEG - 1, 1)

    epool_ref[pl.ds(rim, rows)] = enc[...].reshape(rows, -1).astype(BF16)
    own_enc = epool_ref.at[pl.ds(rim, rows)]
    start_near(own_enc, epool_ref, esend, erecv)
    for link in range(NEXP):
        far(own_enc, epool_ref, link, esend, erecv).start()
    start_near(node_ref, npool_ref, nsend, nrecv)
    start_rest()
    for copy in own_copies:
        copy.wait()

    tile = 512

    def blend(at, size):
        x = jnp.dot(epool_ref[at], we_ref[...], preferred_element_type=F32)
        blended[0:size] = (npool_ref[at].astype(F32) + x).astype(BF16)

    def keys_values(row, size):
        def columns(t, carry):
            cols = pl.ds(pl.multiple_of(D + t * tile, tile), tile)
            y = jnp.dot(blended[0:size], wqkv_ref[:, cols], preferred_element_type=F32).astype(BF16)
            to = pl.ds(pl.multiple_of(t * tile, tile), tile)
            kv[row // BS : (row + size) // BS, :, to] = y.reshape(size // BS, BS, tile)
            return carry

        lax.fori_loop(0, 2 * D // tile, columns, 0)

    blend(pl.ds(rim, rows), rows)

    def queries(t, carry):
        cols = pl.ds(pl.multiple_of(t * tile, tile), tile)
        y = jnp.dot(blended[0:rows], wqkv_ref[:, cols], preferred_element_type=F32).astype(BF16)
        qs[:, cols] = y * jnp.array(1.0 / HD**0.5, BF16)
        return carry

    lax.fori_loop(0, D // tile, queries, 0)
    keys_values(rim, rows)
    for link in range(NEXP):
        for src, dst, send, recv in ((own_enc, epool_ref, esend, erecv), (node_ref, npool_ref, nsend, nrecv)):
            copy = far(src, dst, link, send, recv)
            copy.wait_send()
            copy.wait_recv()
        row = 2 * rim + rows + link * rows
        blend(pl.ds(row, rows), rows)
        keys_values(row, rows)
        if link == 0:
            wait_near(own_enc, epool_ref, esend, erecv)
            wait_near(node_ref, npool_ref, nsend, nrecv)
            for row in (0, rim + rows):
                blend(pl.ds(row, rim), rim)
                keys_values(row, rim)

    pack = 4
    width = pack * HD
    head = lax.broadcasted_iota(jnp.int32, (BS, width), 1) // HD
    keep = [head == h for h in range(pack)]

    def attend(b, carry):
        at = pl.ds(pl.multiple_of(b * BS, BS), BS)
        where = [slots_ref[b, j] for j in range(1 + NL + NEXP)]
        results = []
        for g in range(HEADS // pack):
            cols = slice(g * width, (g + 1) * width)
            vcols = slice(D + g * width, D + (g + 1) * width)
            q = qs[at, cols]
            q = jnp.concatenate([jnp.where(m, q, jnp.zeros_like(q)) for m in keep], axis=0)
            k = jnp.concatenate([kv[w, :, cols] for w in where], axis=0)
            v = jnp.concatenate([kv[w, :, vcols] for w in where], axis=0)
            s = lax.dot_general(q, k, (((1,), (1,)), ((), ())), preferred_element_type=F32)
            p = jnp.exp(s - jnp.max(s, axis=1, keepdims=True))
            p = (p * (1.0 / jnp.sum(p, axis=1, keepdims=True))).astype(BF16)
            o = jnp.dot(p, v, preferred_element_type=F32)
            mine = o[0:BS]
            for h in range(1, pack):
                mine = jnp.where(keep[h], o[h * BS : (h + 1) * BS], mine)
            results.append(mine.astype(BF16))
        for g, result in enumerate(results):
            att[at, g * width : (g + 1) * width] = result
        return carry

    lax.fori_loop(0, count, attend, 0)

    def output(t, carry):
        cols = pl.ds(pl.multiple_of(t * tile, tile), tile)
        out_ref[:, cols] = jnp.dot(att[...], wo_ref[:, cols], preferred_element_type=F32).astype(BF16)
        return carry

    lax.fori_loop(0, D // tile, output, 0)


def on_device(
    n,
    node_feats,
    struct_feats,
    op_blocks,
    laplace_index,
    graph_links,
    expander_slot,
    series_coef,
    encode_weight,
    qkv_weight,
    out_weight,
):
    count = op_blocks.shape[0]
    rows, rim, pch = count * BS, REACH * BS, struct_feats.shape[1]
    pool_rows = rows * (1 + NEXP) + 2 * rim
    vmem = pl.BlockSpec(memory_space=pltpu.VMEM)
    smem = pl.BlockSpec(memory_space=pltpu.SMEM)
    hbm = pl.BlockSpec(memory_space=pl.ANY)
    dma = pltpu.SemaphoreType.DMA
    first_block = lax.axis_index("seq") * count
    own_slot = jnp.arange(count, dtype=jnp.int32)[:, None] + REACH
    graph_slot = graph_links - first_block + REACH
    far_base = count + 2 * REACH + jnp.arange(NEXP, dtype=jnp.int32) * count
    slots = jnp.concatenate([own_slot, graph_slot, far_base[None, :] + expander_slot], axis=1)
    return pl.pallas_call(
        functools.partial(layer_kernel, n),
        out_shape=jax.ShapeDtypeStruct((rows, D), BF16),
        in_specs=[hbm, vmem, vmem, smem, smem, smem, hbm, hbm, hbm],
        out_specs=vmem,
        scratch_shapes=[
            pltpu.VMEM((count + 2 * REACH, BS, 2 * pch), BF16),
            pltpu.VMEM((count + 2 * REACH, BS, 2 * pch), BF16),
            pltpu.VMEM((DEG, 2, REACH, BS, 2 * pch), BF16),
            pltpu.VMEM((count, BS, pch), F32),
            pltpu.VMEM((count, BS, pch), F32),
            pltpu.VMEM((count, BS, pch), F32),
            pltpu.VMEM((count, 2 * BS, NL * BS), BF16),
            pltpu.VMEM((pool_rows, D), BF16),
            pltpu.VMEM((pool_rows, pch), BF16),
            pltpu.VMEM(encode_weight.shape, BF16),
            pltpu.VMEM(qkv_weight.shape, BF16),
            pltpu.VMEM(out_weight.shape, BF16),
            pltpu.VMEM((rows, D), BF16),
            pltpu.VMEM((pool_rows // BS, BS, 2 * D), BF16),
            pltpu.VMEM((rows, D), BF16),
            pltpu.VMEM((rows, D), BF16),
            dma((DEG, 2)),
            dma((DEG, 2)),
            dma((NEXP + 2,)),
            dma((NEXP + 2,)),
            dma((NEXP + 2,)),
            dma((NEXP + 2,)),
            dma((4,)),
        ],
        compiler_params=pltpu.CompilerParams(
            collective_id=0, has_side_effects=True, vmem_limit_bytes=VMEM_LIMIT
        ),
    )(
        node_feats,
        struct_feats,
        op_blocks,
        laplace_index,
        slots,
        series_coef,
        encode_weight,
        qkv_weight,
        out_weight,
    )


def solution(mesh):
    placed = (
        P(("group", "seq"), None),
        P(("group", "seq"), None),
        P(("group", "seq"), None, None, None),
        P(("group", "seq"), None),
        P(("group", "seq"), None),
        P(("group", "seq"), None),
        P(),
        P(),
        P(),
        P(),
    )
    return jax.shard_map(
        functools.partial(on_device, mesh.shape["seq"]),
        mesh=mesh,
        in_specs=placed,
        out_specs=P(("group", "seq"), None),
        check_vma=False,
    )
```
